32 devices in a mesh: grp: 8 (over z, x), blk: 4 (over y, core).
Axes of the slice: x: 2, y: 2, z: 4, core: 2. Of those that a mesh axis runs over, the one named last changes fastest.
Arguments:
- p_tiles: bfloat16 [8, 4, 3, 256, 256], P('grp', 'blk'), may hold values from -0.3984375 to 0.3984375
- pair_slot: int32 [8, 4, 4, 10], P('grp', 'blk'), may hold values from 0 to 2
- pair_panel: int32 [8, 4, 4, 10], P('grp', 'blk'), may hold values from 0 to 23
- pair_out: int32 [8, 4, 4, 10], P('grp', 'blk'), may hold values from 0 to 2
- pair_count: int32 [8, 4, 4], P('grp', 'blk'), may hold values from 1 to 10, as said below
Outputs:
- square: float32 [8, 4, 3, 256, 256], P('grp', 'blk')
- new_tiles: float32 [8, 4, 3, 256, 256], P('grp', 'blk')
The draws below stay inside these ranges and needn't reach their ends.
Inputs may be any that keep to these rules, and one draw needn't show every extreme that they name: `pair_count`: every device has a count of exactly 10 for one source device of its row group.
All inputs are finite; a program needn't handle non-finite values.
Results may differ from the reference program's by a relative error of at most 0.013.
Values may be sent and summed in bfloat16 or wider, within the bound.
A program may use at most 64 MiB of HBM per device.

```python
import jax
import jax.numpy as jnp
from jax import lax

BS = 256
CAP = 3
PER = 10
N_GRP = 8
N_BLK = 4


def draw_pair_count(key, part):
    level_key, count_key = jax.random.split(jax.random.fold_in(key, 17))
    load_level = jax.random.randint(level_key, (N_GRP, N_BLK, 1), 1, PER + 1)
    pair_counts = jax.random.randint(count_key, (N_GRP, N_BLK, N_BLK), 1, load_level + 1)
    group_axis = lax.broadcasted_iota(jnp.int32, (N_GRP, N_BLK, N_BLK), 0)
    member_axis = lax.broadcasted_iota(jnp.int32, (N_GRP, N_BLK, N_BLK), 1)
    source_axis = lax.broadcasted_iota(jnp.int32, (N_GRP, N_BLK, N_BLK), 2)
    full_mask = (group_axis + member_axis) % N_BLK == source_axis
    return jnp.where(full_mask, PER, pair_counts).astype(jnp.int32)


def place_ends(values, stream_key, least, top_value):
    longest = values.shape.index(max(values.shape))
    spots = []
    for shift in (0, 1):
        where = [jax.random.randint(jax.random.fold_in(stream_key, axis), (), 0, length) for axis, length in enumerate(values.shape)]
        where[longest] = (where[longest] + shift) % values.shape[longest]
        spots.append(tuple(where))
    return values.at[spots[0]].set(least).at[spots[1]].set(top_value)


def level_of(own_key, dims, cuts, low, largest):
    factor_of = 1.0
    for position, parts in cuts:
        heights = jax.random.uniform(jax.random.fold_in(jax.random.fold_in(own_key, 6), position), (parts,), jnp.float32, low / len(cuts), largest / len(cuts))
        factor_of = factor_of * jnp.repeat(jnp.exp(heights), dims[position] // parts).reshape((-1,) + (1,) * (len(dims) - 1 - position))
    return factor_of


def centred(stream_key, shape, spread, reach, cuts=(), held_as=jnp.bfloat16):
    drawn = spread * jax.random.normal(stream_key, shape, jnp.float32)
    if cuts:
        drawn = drawn * level_of(stream_key, shape, cuts, -0.22, 0.18)
    return jnp.clip(drawn, -reach, reach).astype(held_as)


def setup_inputs(seed: int = 0) -> dict:
    streams_of = jax.random.split(jax.random.key(seed), 6)
    p_tiles = centred(streams_of[0], (N_GRP, N_BLK, CAP, BS, BS), 0.0625, 0.3984375, ((0, 8), (1, 4)))
    pair_slot = place_ends(jax.random.randint(streams_of[1], (N_GRP, N_BLK, N_BLK, PER), 0, CAP), jax.random.fold_in(streams_of[1], 1), 0, CAP - 1).astype(jnp.int32)
    pair_panel = place_ends(jax.random.randint(streams_of[2], (N_GRP, N_BLK, N_BLK, PER), 0, N_GRP * CAP), jax.random.fold_in(streams_of[2], 1), 0, (N_GRP * CAP) - 1).astype(jnp.int32)
    pair_out = place_ends(jax.random.randint(streams_of[3], (N_GRP, N_BLK, N_BLK, PER), 0, CAP), jax.random.fold_in(streams_of[3], 1), 0, CAP - 1).astype(jnp.int32)
    pair_count = draw_pair_count(jax.random.fold_in(streams_of[5], 71), 0)
    return dict(p_tiles=p_tiles, pair_slot=pair_slot, pair_panel=pair_panel, pair_out=pair_out, pair_count=pair_count)


def device_products(group_tiles, panel_tiles, slot_list, panel_list, out_list, count_list):
    def per_source(running, scanned):
        source_tiles, slot_row, panel_row, out_row, pair_total = scanned
        left_tiles = source_tiles[slot_row].astype(jnp.float32)
        right_tiles = panel_tiles[panel_row].astype(jnp.float32)
        products = jnp.einsum('pij,pjk->pik', left_tiles, right_tiles)
        live_mask = (jnp.arange(PER) < pair_total).astype(jnp.float32)
        one_hot = (out_row[:, None] == jnp.arange(CAP)[None, :]).astype(jnp.float32) * live_mask[:, None]
        return running + jnp.einsum('po,pik->oik', one_hot, products), None

    start_sum = jnp.zeros((CAP, BS, BS), jnp.float32)
    result, _ = lax.scan(per_source, start_sum, (group_tiles, slot_list, panel_list, out_list, count_list))
    return result


def multiply_round(left_all, right_all, pair_slot, pair_panel, pair_out, pair_count):
    def per_device(device_index):
        row_group = device_index // N_BLK
        cycle_pos = device_index % N_BLK
        panel_tiles = right_all[:, cycle_pos].reshape(N_GRP * CAP, BS, BS)
        return device_products(left_all[row_group], panel_tiles, pair_slot[row_group, cycle_pos],
                               pair_panel[row_group, cycle_pos], pair_out[row_group, cycle_pos],
                               pair_count[row_group, cycle_pos])

    stacked = lax.map(per_device, jnp.arange(N_GRP * N_BLK))
    return stacked.reshape(N_GRP, N_BLK, CAP, BS, BS)


def reference(p_tiles, pair_slot, pair_panel, pair_out, pair_count):
    square = multiply_round(p_tiles, p_tiles, pair_slot, pair_panel, pair_out, pair_count)
    square_half = square.astype(jnp.bfloat16)
    cube_tiles = multiply_round(square_half, p_tiles, pair_slot, pair_panel, pair_out, pair_count)
    new_tiles = 3.0 * square - 2.0 * cube_tiles
    return square, new_tiles
```

```python
import functools

import jax
import jax.numpy as jnp
from jax import lax
from jax.experimental import pallas as pl
from jax.experimental.pallas import tpu as pltpu
from jax.sharding import PartitionSpec as P

MESH = pl.DeviceIdType.MESH
VMEM = pl.BlockSpec(memory_space=pltpu.VMEM)
SMEM = pl.BlockSpec(memory_space=pltpu.SMEM)


def remote(ref, block, cap, send_sem, recv_sem, target):
    part = ref.at[pl.ds(block * cap, cap)]
    return pltpu.make_async_remote_copy(
        src_ref=part, dst_ref=part, send_sem=send_sem, recv_sem=recv_sem,
        device_id=target, device_id_type=MESH,
    )


def greet(targets):
    barrier = pltpu.get_barrier_semaphore()
    for present, target in targets:
        @pl.when(present)
        def _():
            pl.semaphore_signal(barrier, inc=1, device_id=target, device_id_type=MESH)
    total = sum(jnp.where(present, 1, 0) for present, _ in targets)
    pl.semaphore_wait(barrier, total)


class Group:
    def __init__(self, n_blk, cap):
        self.cap = cap
        self.g = lax.axis_index("grp")
        self.b = lax.axis_index("blk")
        self.chips = n_blk // 2
        self.q, self.core = self.b // 2, self.b % 2
        self.mate = (self.g, 2 * self.q + 1 - self.core)

    def peers(self):
        yes = self.b >= 0
        out = [(yes, self.mate)]
        for d in range(1, self.chips):
            out.append((yes, (self.g, self.chip(d))))
        return out

    def chip(self, d):
        return 2 * ((self.q + d) % self.chips) + self.core

    def source(self, d):
        return 2 * ((self.q + self.chips - d) % self.chips) + self.core

    def far(self, ref, sems, d):
        return remote(ref, self.b, self.cap, sems[0].at[d], sems[1].at[d], (self.g, self.chip(d)))

    def near(self, ref, sems, d):
        n = self.chips
        return remote(ref, self.source(d), self.cap, sems[0].at[n + d], sems[1].at[n + d], self.mate)

    def start(self, ref, sems):
        for d in range(1, self.chips):
            self.far(ref, sems, d).start()
        self.near(ref, sems, 0).start()

    def forward(self, ref, sems):
        for d in range(1, self.chips):
            self.far(ref, sems, d).wait_recv()
            self.near(ref, sems, d).start()

    def finish(self, ref, sems):
        for d in range(self.chips):
            self.near(ref, sems, d).wait_recv()

    def drain(self, ref, sems):
        for d in range(1, self.chips):
            self.far(ref, sems, d).wait_send()
        for d in range(self.chips):
            self.near(ref, sems, d).wait_send()


class Panel:
    def __init__(self, n_grp, cap):
        self.cap = cap
        self.b = lax.axis_index("blk")
        g = lax.axis_index("grp")
        self.nz = n_grp // 2
        self.z, self.x = g // 2, g % 2

    def peers(self):
        yes = self.b >= 0
        return [
            (self.z < self.nz - 1, self.at(self.z + 1)),
            (self.z > 0, self.at(self.z - 1)),
            (yes, (2 * self.z + 1 - self.x, self.b)),
        ]

    def at(self, z):
        return (2 * z + self.x, self.b)

    def line(self, ref, sems, way, k):
        step = 1 if way == 0 else -1
        block = self.z - step * k
        i = way * self.nz + k
        return remote(ref, 2 * block + self.x, self.cap, sems[0].at[i], sems[1].at[i], self.at(self.z + step))

    def cross(self, ref, sems, z):
        i = 2 * self.nz + z
        return remote(ref, 2 * z + self.x, self.cap, sems[0].at[i], sems[1].at[i], (2 * self.z + 1 - self.x, self.b))

    def sends(self, way, k):
        if way == 0:
            return jnp.logical_and(self.z < self.nz - 1, self.z >= k)
        return jnp.logical_and(self.z > 0, self.nz - 1 - self.z >= k)

    def gets(self, way, k):
        return self.z >= k + 1 if way == 0 else self.nz - 1 - self.z >= k + 1

    def start(self, ref, sems):
        for way in (0, 1):
            @pl.when(self.sends(way, 0))
            def _():
                self.line(ref, sems, way, 0).start()
        self.cross(ref, sems, self.z).start()

    def step(self, ref, sems, k):
        for way in (0, 1):
            @pl.when(self.gets(way, k))
            def _():
                self.line(ref, sems, way, k).wait_recv()
                self.cross(ref, sems, self.z - (k + 1 if way == 0 else -(k + 1))).start()

                @pl.when(self.sends(way, k + 1))
                def _():
                    self.line(ref, sems, way, k + 1).start()

    def finish(self, ref, sems):
        for z in range(self.nz):
            self.cross(ref, sems, z).wait_recv()

    def drain(self, ref, sems):
        for z in range(self.nz):
            self.cross(ref, sems, z).wait_send()
        for k in range(self.nz):
            for way in (0, 1):
                @pl.when(self.sends(way, k))
                def _():
                    self.line(ref, sems, way, k).wait_send()


def gather_kernel(n_grp, n_blk, p_ref, panel_ref, left_ref, panel, left, ps, pr, gs, gr, out_sems):
    cap = p_ref.shape[0]
    wide, group = Panel(n_grp, cap), Group(n_blk, cap)
    panel[pl.ds((2 * wide.z + wide.x) * cap, cap)] = p_ref[...]
    left[pl.ds(group.b * cap, cap)] = p_ref[...]
    greet(wide.peers() + group.peers())
    wide.start(panel, (ps, pr))
    group.start(left, (gs, gr))
    for k in range(wide.nz - 1):
        wide.step(panel, (ps, pr), k)
        if k == 0:
            group.forward(left, (gs, gr))
            group.finish(left, (gs, gr))
    wide.finish(panel, (ps, pr))
    first = pltpu.make_async_copy(panel, panel_ref, out_sems.at[0])
    second = pltpu.make_async_copy(left, left_ref, out_sems.at[1])
    first.start()
    second.start()
    wide.drain(panel, (ps, pr))
    group.drain(left, (gs, gr))
    first.wait()
    second.wait()


def exchange_kernel(n_blk, p_ref, left_ref, left, gs, gr, out_sem):
    cap = p_ref.shape[0]
    group = Group(n_blk, cap)
    left[pl.ds(group.b * cap, cap)] = p_ref[...]
    greet(group.peers())
    group.start(left, (gs, gr))
    group.forward(left, (gs, gr))
    group.finish(left, (gs, gr))
    copy = pltpu.make_async_copy(left, left_ref, out_sem)
    copy.start()
    group.drain(left, (gs, gr))
    copy.wait()


def accumulate(acc, left_ref, panel_ref, slot, pick, out, count):
    acc[...] = jnp.zeros_like(acc)
    n_blk, cap = count.shape[0], acc.shape[0]

    def source(c, carry):
        def pair(e, inner):
            lhs = left_ref[c * cap + slot[c, e]]
            rhs = panel_ref[pick[c, e]]
            o = out[c, e]
            acc[o] += jnp.dot(lhs, rhs, preferred_element_type=jnp.float32)
            return inner

        return lax.fori_loop(0, count[c], pair, carry)

    lax.fori_loop(0, n_blk, source, 0)


def square_kernel(slot, pick, out, count, left_ref, panel_ref, square_ref, half_ref):
    accumulate(square_ref, left_ref, panel_ref, slot, pick, out, count)
    half_ref[...] = square_ref[...].astype(half_ref.dtype)


def cube_kernel(slot, pick, out, count, left_ref, panel_ref, square_ref, new_ref):
    accumulate(new_ref, left_ref, panel_ref, slot, pick, out, count)
    new_ref[...] = 3.0 * square_ref[...] - 2.0 * new_ref[...]


def local(n_grp, n_blk, p_tiles, pair_slot, pair_panel, pair_out, pair_count):
    held = p_tiles[0, 0]
    lists = (pair_slot[0, 0], pair_panel[0, 0], pair_out[0, 0], pair_count[0, 0])
    cap, bs, _ = held.shape
    nz, chips = n_grp // 2, n_blk // 2
    dma = pltpu.SemaphoreType.DMA
    panel_type = jax.ShapeDtypeStruct((n_grp * cap, bs, bs), held.dtype)
    left_type = jax.ShapeDtypeStruct((n_blk * cap, bs, bs), held.dtype)
    tile_type = jax.ShapeDtypeStruct((cap, bs, bs), jnp.float32)
    half_type = jax.ShapeDtypeStruct((cap, bs, bs), held.dtype)
    anywhere = pl.BlockSpec(memory_space=pl.ANY)
    limit = 40 * 2**20
    panel, left = pl.pallas_call(
        functools.partial(gather_kernel, n_grp, n_blk),
        out_shape=(panel_type, left_type),
        in_specs=[VMEM],
        out_specs=(anywhere, anywhere),
        scratch_shapes=[
            pltpu.VMEM(panel_type.shape, held.dtype),
            pltpu.VMEM(left_type.shape, held.dtype),
            dma((3 * nz,)), dma((3 * nz,)), dma((2 * chips,)), dma((2 * chips,)), dma((2,)),
        ],
        compiler_params=pltpu.CompilerParams(
            collective_id=0, has_side_effects=True, vmem_limit_bytes=limit),
    )(held)
    square, half = pl.pallas_call(
        square_kernel,
        out_shape=(tile_type, half_type),
        in_specs=[SMEM] * 4 + [VMEM] * 2,
        out_specs=(VMEM, VMEM),
        compiler_params=pltpu.CompilerParams(vmem_limit_bytes=limit),
    )(*lists, left, panel)
    left2 = pl.pallas_call(
        functools.partial(exchange_kernel, n_blk),
        out_shape=left_type,
        in_specs=[VMEM],
        out_specs=anywhere,
        scratch_shapes=[
            pltpu.VMEM(left_type.shape, held.dtype), dma((2 * chips,)), dma((2 * chips,)), dma,
        ],
        compiler_params=pltpu.CompilerParams(
            collective_id=1, has_side_effects=True, vmem_limit_bytes=limit),
    )(half)
    new = pl.pallas_call(
        cube_kernel,
        out_shape=tile_type,
        in_specs=[SMEM] * 4 + [VMEM] * 3,
        out_specs=VMEM,
        compiler_params=pltpu.CompilerParams(vmem_limit_bytes=limit),
    )(*lists, left2, panel, square)
    return square[None, None], new[None, None]


def solution(mesh):
    in_specs = (
        P("grp", "blk", None, None, None),
        P("grp", "blk", None, None),
        P("grp", "blk", None, None),
        P("grp", "blk", None, None),
        P("grp", "blk", None),
    )
    out_specs = (P("grp", "blk", None, None, None), P("grp", "blk", None, None, None))
    body = functools.partial(local, mesh.shape["grp"], mesh.shape["blk"])
    return jax.shard_map(body, mesh=mesh, in_specs=in_specs, out_specs=out_specs, check_vma=False)
```

```python
import functools

import jax
import jax.numpy as jnp
from jax import lax
from jax.experimental import pallas as pl
from jax.experimental.pallas import tpu as pltpu
from jax.sharding import PartitionSpec as P

MESH = pl.DeviceIdType.MESH
HBM = pl.BlockSpec(memory_space=pl.ANY)
SKEW = 1


def remote(ref, first, length, send_sem, recv_sem, target):
    part = ref.at[pl.ds(first, length)]
    return pltpu.make_async_remote_copy(
        src_ref=part, dst_ref=part, send_sem=send_sem, recv_sem=recv_sem,
        device_id=target, device_id_type=MESH,
    )


def greet(targets):
    barrier = pltpu.get_barrier_semaphore()
    for present, target in targets:
        @pl.when(present)
        def _():
            pl.semaphore_signal(barrier, inc=1, device_id=target, device_id_type=MESH)
    total = sum(jnp.where(present, 1, 0) for present, _ in targets)
    pl.semaphore_wait(barrier, total)


class Group:
    def __init__(self, n_blk, cap):
        self.cap = cap
        self.g = lax.axis_index("grp")
        self.b = lax.axis_index("blk")
        self.chips = n_blk // 2
        self.q, self.core = self.b // 2, self.b % 2
        self.mate = (self.g, 2 * self.q + 1 - self.core)

    def peers(self):
        yes = self.b >= 0
        out = [(yes, self.mate)]
        for d in range(1, self.chips):
            out.append((yes, (self.g, self.chip(d))))
        return out

    def chip(self, d):
        return 2 * ((self.q + d) % self.chips) + self.core

    def source(self, d):
        return 2 * ((self.q + self.chips - d) % self.chips) + self.core

    def far(self, ref, sems, d):
        return remote(ref, self.b * self.cap, self.cap, sems[0].at[d], sems[1].at[d], (self.g, self.chip(d)))

    def near(self, ref, sems, d):
        n = self.chips
        return remote(ref, self.source(d) * self.cap, self.cap, sems[0].at[n + d], sems[1].at[n + d], self.mate)

    def start(self, ref, sems):
        for d in range(1, self.chips):
            self.far(ref, sems, d).start()
        self.near(ref, sems, 0).start()

    def forward(self, ref, sems):
        for d in range(1, self.chips):
            self.far(ref, sems, d).wait_recv()
            self.near(ref, sems, d).start()

    def finish(self, ref, sems):
        for d in range(self.chips):
            self.near(ref, sems, d).wait_recv()

    def drain(self, ref, sems):
        for d in range(1, self.chips):
            self.far(ref, sems, d).wait_send()
        for d in range(self.chips):
            self.near(ref, sems, d).wait_send()


class Panel:
    def __init__(self, n_grp, halves):
        self.halves = halves
        self.b = lax.axis_index("blk")
        g = lax.axis_index("grp")
        self.nz = n_grp // 2
        self.z, self.x = g // 2, g % 2
        self.across = (2 * self.z + 1 - self.x, self.b)

    def peers(self):
        yes = self.b >= 0
        return [
            (self.z < self.nz - 1, self.at(self.z + 1)),
            (self.z > 0, self.at(self.z - 1)),
            (yes, self.across),
        ]

    def at(self, z):
        return (2 * z + self.x, self.b)

    def copy(self, ref, sems, i, block, tail, target):
        most = self.halves - 1
        first = block * self.halves + (most if tail else 0)
        return remote(ref, first, 1 if tail else most, sems[0].at[i], sems[1].at[i], target)

    def line(self, ref, sems, kind, way, k):
        step = 1 if way == 0 else -1
        column = 1 - self.x if kind == 2 else self.x
        i = (2 * kind + way) * self.nz + k
        return self.copy(ref, sems, i, 2 * (self.z - step * k) + column, kind > 0, self.at(self.z + step))

    def cross(self, ref, sems, z):
        return self.copy(ref, sems, 6 * self.nz + z, 2 * z + self.x, False, self.across)

    def cross_tail(self, ref, sems):
        return self.copy(ref, sems, 7 * self.nz, 2 * self.z + self.x, True, self.across)

    def sends(self, way, k):
        if way == 0:
            return jnp.logical_and(self.z < self.nz - 1, self.z >= k)
        return jnp.logical_and(self.z > 0, self.nz - 1 - self.z >= k)

    def gets(self, way, k):
        return self.z >= k + 1 if way == 0 else self.nz - 1 - self.z >= k + 1

    def start(self, ref, sems):
        self.cross_tail(ref, sems).start()
        self.cross(ref, sems, self.z).start()
        for way in (0, 1):
            @pl.when(self.sends(way, 0))
            def _():
                self.line(ref, sems, 0, way, 0).start()
                self.line(ref, sems, 1, way, 0).start()
        self.cross_tail(ref, sems).wait_recv()
        for way in (0, 1):
            @pl.when(self.sends(way, 0))
            def _():
                self.line(ref, sems, 2, way, 0).start()

    def step(self, ref, sems, k):
        for way in (0, 1):
            @pl.when(self.gets(way, k))
            def _():
                for kind in range(3):
                    self.line(ref, sems, kind, way, k).wait_recv()
                    if kind == 0:
                        self.cross(ref, sems, self.z - (k + 1 if way == 0 else -(k + 1))).start()

                    @pl.when(self.sends(way, k + 1))
                    def _():
                        self.line(ref, sems, kind, way, k + 1).start()

    def finish(self, ref, sems):
        for z in range(self.nz):
            self.cross(ref, sems, z).wait_recv()

    def drain(self, ref, sems):
        self.cross_tail(ref, sems).wait_send()
        for z in range(self.nz):
            self.cross(ref, sems, z).wait_send()
        for k in range(self.nz):
            for way in (0, 1):
                @pl.when(self.sends(way, k))
                def _():
                    for kind in range(3):
                        self.line(ref, sems, kind, way, k).wait_send()


def add_products(acc, lists, left_ref, right_tile):
    slot, pick, out, count = lists
    n_blk, per = slot.shape
    cap = acc.shape[0]
    dtype = left_ref.dtype

    def source(c, carry):
        total = count[0, c]
        lefts, rights = [], []
        for e in range(per):
            tile = left_ref[c * cap + slot[c, e]]
            enters = jnp.where(e < total, out[c, e], cap)
            rows = []
            for o in range(cap):
                weight = jnp.where(enters == o, 1.0, 0.0)
                rows.append(tile * jnp.full((1, tile.shape[1]), weight, jnp.float32).astype(dtype))
            lefts.append(jnp.concatenate(rows, axis=0))
            rights.append(right_tile(pick[c, e]))
        product = jnp.dot(
            jnp.concatenate(lefts, axis=1), jnp.concatenate(rights, axis=0),
            preferred_element_type=jnp.float32,
        )
        acc[...] += product.reshape(acc.shape)
        return carry

    lax.fori_loop(0, n_blk, source, 0)


def kernel(n_grp, n_blk, *refs):
    p_hbm, lists_hbm = refs[0], refs[1:5]
    square_hbm, new_hbm = refs[5:7]
    panels, left, halves, squares, cube = refs[7:9], refs[9], refs[10:12], refs[12:14], refs[14]
    lists = refs[15:19]
    ps, pr, gs, gr, local_sems = refs[19:]
    cap, bs, _ = p_hbm.shape
    w = bs // 2
    wide, group = Panel(n_grp, 2 * cap), Group(n_blk, cap)
    panel_sems = [(ps.at[j], pr.at[j]) for j in range(2)]
    group_sems = [(gs.at[j], gr.at[j]) for j in range(3)]

    own = pl.ds(group.b * cap, cap)
    fetch = pltpu.make_async_copy(p_hbm, left.at[own], local_sems.at[0])
    fetch.start()
    list_copies = [
        pltpu.make_async_copy(source, target, local_sems.at[1 + i])
        for i, (source, target) in enumerate(zip(lists_hbm, lists))
    ]
    for copy in list_copies:
        copy.start()
    fetch.wait()
    mine = left[own]
    first = (2 * wide.z + wide.x) * 2 * cap
    for j in range(2):
        panels[j][pl.ds(first, 2 * cap)] = mine[:, :, j * w:(j + 1) * w].reshape(2 * cap, w, w)
    greet(wide.peers() + group.peers())

    for t in range(wide.nz + SKEW):
        for j in range(2):
            k = t - SKEW * j
            if k == 0:
                wide.start(panels[j], panel_sems[j])
                if j == 0:
                    group.start(left, group_sems[2])
            elif 0 < k < wide.nz:
                wide.step(panels[j], panel_sems[j], k - 1)
        if t == 1:
            group.forward(left, group_sems[2])
    group.finish(left, group_sems[2])
    for copy in list_copies:
        copy.wait()

    square_copies = []
    for j in range(2):
        wide.finish(panels[j], panel_sems[j])
        squares[j][...] = jnp.zeros_like(squares[j])
        add_products(
            squares[j], lists, left, lambda t, j=j: panels[j][pl.ds(2 * t, 2)].reshape(bs, w))
        halves[j][own] = squares[j][...].astype(left.dtype)
        group.start(halves[j], group_sems[j])
        square_copies.append(pltpu.make_async_copy(
            squares[j], square_hbm.at[:, :, pl.ds(j * w, w)], local_sems.at[5 + j]))
        square_copies[j].start()
    cube[...] = jnp.zeros_like(cube)
    for j in range(2):
        group.forward(halves[j], group_sems[j])
        group.finish(halves[j], group_sems[j])
        add_products(
            cube, lists, halves[j],
            lambda t, j=j: jnp.concatenate([panels[0][2 * t + j], panels[1][2 * t + j]], axis=1))
    for j in range(2):
        cols = slice(j * w, (j + 1) * w)
        cube[:, :, cols] = 3.0 * squares[j][...] - 2.0 * cube[:, :, cols]
    last = pltpu.make_async_copy(cube, new_hbm, local_sems.at[7])
    last.start()
    for j in range(2):
        wide.drain(panels[j], panel_sems[j])
        square_copies[j].wait()
    for j, ref in enumerate((halves[0], halves[1], left)):
        group.drain(ref, group_sems[j])
    last.wait()


def local(n_grp, n_blk, p_tiles, pair_slot, pair_panel, pair_out, pair_count):
    held = p_tiles[0, 0]
    lists = (pair_slot[0, 0], pair_panel[0, 0], pair_out[0, 0], pair_count[0])
    cap, bs, _ = held.shape
    nz, chips, w = n_grp // 2, n_blk // 2, bs // 2
    dma = pltpu.SemaphoreType.DMA
    tile_type = jax.ShapeDtypeStruct((cap, bs, bs), jnp.float32)
    square, new = pl.pallas_call(
        functools.partial(kernel, n_grp, n_blk),
        out_shape=(tile_type, tile_type),
        in_specs=[HBM] * 5,
        out_specs=(HBM, HBM),
        scratch_shapes=[pltpu.VMEM((n_grp * cap * 2, w, w), held.dtype)] * 2
        + [pltpu.VMEM((n_blk * cap, bs, bs), held.dtype)]
        + [pltpu.VMEM((n_blk * cap, bs, w), held.dtype)] * 2
        + [pltpu.VMEM((cap, bs, w), jnp.float32)] * 2
        + [pltpu.VMEM((cap, bs, bs), jnp.float32)]
        + [pltpu.SMEM(x.shape, x.dtype) for x in lists]
        + [dma((2, 7 * nz + 1))] * 2 + [dma((3, 2 * chips))] * 2 + [dma((8,))],
        compiler_params=pltpu.CompilerParams(
            collective_id=0, has_side_effects=True, vmem_limit_bytes=48 * 2**20),
    )(held, *lists)
    return square[None, None], new[None, None]


def solution(mesh):
    in_specs = (
        P("grp", "blk", None, None, None),
        P("grp", "blk", None, None),
        P("grp", "blk", None, None),
        P("grp", "blk", None, None),
        P("grp", "blk", None),
    )
    out_specs = (P("grp", "blk", None, None, None), P("grp", "blk", None, None, None))
    body = functools.partial(local, mesh.shape["grp"], mesh.shape["blk"])
    return jax.shard_map(body, mesh=mesh, in_specs=in_specs, out_specs=out_specs, check_vma=False)
```

```python
import functools

import jax
import jax.numpy as jnp
from jax import lax
from jax.experimental import pallas as pl
from jax.experimental.pallas import tpu as pltpu
from jax.sharding import PartitionSpec as P

MESH = pl.DeviceIdType.MESH
HBM = pl.BlockSpec(memory_space=pl.ANY)


def remote(ref, first, length, send_sem, recv_sem, target):
    part = ref.at[pl.ds(first, length)]
    return pltpu.make_async_remote_copy(
        src_ref=part, dst_ref=part, send_sem=send_sem, recv_sem=recv_sem,
        device_id=target, device_id_type=MESH,
    )


def greet(targets):
    barrier = pltpu.get_barrier_semaphore()
    for present, target in targets:
        @pl.when(present)
        def _():
            pl.semaphore_signal(barrier, inc=1, device_id=target, device_id_type=MESH)
    total = sum(jnp.where(present, 1, 0) for present, _ in targets)
    pl.semaphore_wait(barrier, total)


class Group:
    def __init__(self, n_blk, cap):
        self.cap = cap
        self.g = lax.axis_index("grp")
        self.b = lax.axis_index("blk")
        self.chips = n_blk // 2
        self.q, self.core = self.b // 2, self.b % 2
        self.mate = (self.g, 2 * self.q + 1 - self.core)

    def peers(self):
        yes = self.b >= 0
        out = [(yes, self.mate)]
        for d in range(1, self.chips):
            out.append((yes, (self.g, self.chip(d))))
        return out

    def chip(self, d):
        return 2 * ((self.q + d) % self.chips) + self.core

    def source(self, d):
        return 2 * ((self.q + self.chips - d) % self.chips) + self.core

    def far(self, ref, sems, d):
        return remote(ref, self.b * self.cap, self.cap, sems[0].at[d], sems[1].at[d], (self.g, self.chip(d)))

    def near(self, ref, sems, d):
        n = self.chips
        return remote(ref, self.source(d) * self.cap, self.cap, sems[0].at[n + d], sems[1].at[n + d], self.mate)

    def start(self, ref, sems):
        for d in range(1, self.chips):
            self.far(ref, sems, d).start()
        self.near(ref, sems, 0).start()

    def forward(self, ref, sems):
        for d in range(1, self.chips):
            self.far(ref, sems, d).wait_recv()
            self.near(ref, sems, d).start()

    def finish(self, ref, sems):
        for d in range(self.chips):
            self.near(ref, sems, d).wait_recv()

    def drain(self, ref, sems):
        for d in range(1, self.chips):
            self.far(ref, sems, d).wait_send()
        for d in range(self.chips):
            self.near(ref, sems, d).wait_send()


class Panel:
    def __init__(self, n_grp, size):
        self.size = size
        self.b = lax.axis_index("blk")
        g = lax.axis_index("grp")
        self.nz = n_grp // 2
        self.z, self.x = g // 2, g % 2
        self.across = (2 * self.z + 1 - self.x, self.b)

    def peers(self):
        yes = self.b >= 0
        return [
            (self.z < self.nz - 1, self.at(self.z + 1)),
            (self.z > 0, self.at(self.z - 1)),
            (yes, self.across),
        ]

    def at(self, z):
        return (2 * z + self.x, self.b)

    def copy(self, ref, sems, i, z, target):
        first = (2 * z + self.x) * self.size
        return remote(ref, first, self.size, sems[0].at[i], sems[1].at[i], target)

    def line(self, ref, sems, way, k):
        step = 1 if way == 0 else -1
        return self.copy(ref, sems, way * self.nz + k, self.z - step * k, self.at(self.z + step))

    def cross(self, ref, sems, z):
        return self.copy(ref, sems, 2 * self.nz + z, z, self.across)

    def sends(self, way, k):
        if way == 0:
            return jnp.logical_and(self.z < self.nz - 1, self.z >= k)
        return jnp.logical_and(self.z > 0, self.nz - 1 - self.z >= k)

    def gets(self, way, k):
        return self.z >= k + 1 if way == 0 else self.nz - 1 - self.z >= k + 1

    def start(self, ref, sems):
        self.cross(ref, sems, self.z).start()
        for way in (0, 1):
            @pl.when(self.sends(way, 0))
            def _():
                self.line(ref, sems, way, 0).start()

    def step(self, ref, sems, k):
        for way in (0, 1):
            @pl.when(self.gets(way, k))
            def _():
                self.line(ref, sems, way, k).wait_recv()
                self.cross(ref, sems, self.z - (k + 1 if way == 0 else -(k + 1))).start()

                @pl.when(self.sends(way, k + 1))
                def _():
                    self.line(ref, sems, way, k + 1).start()

    def finish(self, ref, sems):
        for z in range(self.nz):
            self.cross(ref, sems, z).wait_recv()

    def drain(self, ref, sems):
        for z in range(self.nz):
            self.cross(ref, sems, z).wait_send()
        for k in range(self.nz):
            for way in (0, 1):
                @pl.when(self.sends(way, k))
                def _():
                    self.line(ref, sems, way, k).wait_send()


def add_products(acc, lists, left_tile, right_tile):
    slot, pick, out, count = lists
    n_blk, per = slot.shape
    cap = acc.shape[0]

    def source(c, carry):
        total = count[0, c]
        sums = [acc[o] for o in range(cap)]
        for e in range(per):
            product = jnp.dot(
                left_tile(c * cap + slot[c, e]), right_tile(pick[c, e]),
                preferred_element_type=jnp.float32,
            )
            enters = jnp.where(e < total, out[c, e], cap)
            for o in range(cap):
                sums[o] = sums[o] + jnp.where(enters == o, 1.0, 0.0) * product
        for o in range(cap):
            acc[o] = sums[o]
        return carry

    lax.fori_loop(0, n_blk, source, 0)


def kernel(n_grp, n_blk, *refs):
    p_hbm, lists_hbm = refs[0], refs[1:5]
    square_hbm, new_hbm = refs[5:7]
    panels, left, halves, squares, cube = refs[7:9], refs[9], refs[10:12], refs[12:14], refs[14]
    lists = refs[15:19]
    ps, pr, gs, gr, local_sems = refs[19:]
    cap, bs, _ = p_hbm.shape
    w = bs // 2
    wide, group = Panel(n_grp, 2 * cap), Group(n_blk, cap)
    panel_sems = [(ps.at[j], pr.at[j]) for j in range(2)]
    group_sems = [(gs.at[j], gr.at[j]) for j in range(3)]

    own = pl.ds(group.b * cap, cap)
    fetch = pltpu.make_async_copy(p_hbm, left.at[own], local_sems.at[0])
    fetch.start()
    list_copies = [
        pltpu.make_async_copy(source, target, local_sems.at[1 + i])
        for i, (source, target) in enumerate(zip(lists_hbm, lists))
    ]
    for copy in list_copies:
        copy.start()
    fetch.wait()
    mine = left[own]
    first = (2 * wide.z + wide.x) * 2 * cap
    for j in range(2):
        panels[j][pl.ds(first, 2 * cap)] = mine[:, :, j * w:(j + 1) * w].reshape(2 * cap, w, w)
    greet(wide.peers() + group.peers())

    square_copies = []

    def square_chunk(j):
        wide.finish(panels[j], panel_sems[j])
        squares[j][...] = jnp.zeros_like(squares[j])
        add_products(
            squares[j], lists, lambda i: left[i],
            lambda t: panels[j][pl.ds(2 * t, 2)].reshape(bs, w))
        halves[j][own] = squares[j][...].astype(left.dtype)
        group.start(halves[j], group_sems[j])
        square_copies.append(pltpu.make_async_copy(
            squares[j], square_hbm.at[:, :, pl.ds(j * w, w)], local_sems.at[5 + j]))
        square_copies[j].start()

    wide.start(panels[0], panel_sems[0])
    group.start(left, group_sems[2])
    for k in range(wide.nz - 1):
        wide.step(panels[0], panel_sems[0], k)
        if k == 0:
            wide.start(panels[1], panel_sems[1])
        else:
            wide.step(panels[1], panel_sems[1], k - 1)
    group.forward(left, group_sems[2])
    group.finish(left, group_sems[2])
    for copy in list_copies:
        copy.wait()
    square_chunk(0)
    wide.step(panels[1], panel_sems[1], wide.nz - 2)
    group.forward(halves[0], group_sems[0])
    square_chunk(1)
    cube[...] = jnp.zeros_like(cube)
    group.forward(halves[1], group_sems[1])
    for j in range(2):
        group.finish(halves[j], group_sems[j])

    def right_whole(t):
        return jnp.concatenate(
            [panel[pl.ds(2 * t, 2)].reshape(bs, w) for panel in panels], axis=1)

    add_products(
        cube, lists, lambda i: jnp.concatenate([half[i] for half in halves], axis=1), right_whole)
    for j in range(2):
        cols = slice(j * w, (j + 1) * w)
        cube[:, :, cols] = 3.0 * squares[j][...] - 2.0 * cube[:, :, cols]
    last = pltpu.make_async_copy(cube, new_hbm, local_sems.at[7])
    last.start()
    for j in range(2):
        wide.drain(panels[j], panel_sems[j])
        square_copies[j].wait()
    for j, ref in enumerate((halves[0], halves[1], left)):
        group.drain(ref, group_sems[j])
    last.wait()


def local(n_grp, n_blk, p_tiles, pair_slot, pair_panel, pair_out, pair_count):
    held = p_tiles[0, 0]
    lists = (pair_slot[0, 0], pair_panel[0, 0], pair_out[0, 0], pair_count[0])
    cap, bs, _ = held.shape
    nz, chips, w = n_grp // 2, n_blk // 2, bs // 2
    dma = pltpu.SemaphoreType.DMA
    tile_type = jax.ShapeDtypeStruct((cap, bs, bs), jnp.float32)
    square, new = pl.pallas_call(
        functools.partial(kernel, n_grp, n_blk),
        out_shape=(tile_type, tile_type),
        in_specs=[HBM] * 5,
        out_specs=(HBM, HBM),
        scratch_shapes=[pltpu.VMEM((n_grp * cap * 2, w, w), held.dtype)] * 2
        + [pltpu.VMEM((n_blk * cap, bs, bs), held.dtype)]
        + [pltpu.VMEM((n_blk * cap, bs, w), held.dtype)] * 2
        + [pltpu.VMEM((cap, bs, w), jnp.float32)] * 2
        + [pltpu.VMEM((cap, bs, bs), jnp.float32)]
        + [pltpu.SMEM(x.shape, x.dtype) for x in lists]
        + [dma((2, 3 * nz))] * 2 + [dma((3, 2 * chips))] * 2 + [dma((8,))],
        compiler_params=pltpu.CompilerParams(
            collective_id=0, has_side_effects=True, vmem_limit_bytes=48 * 2**20),
    )(held, *lists)
    return square[None, None], new[None, None]


def solution(mesh):
    in_specs = (
        P("grp", "blk", None, None, None),
        P("grp", "blk", None, None),
        P("grp", "blk", None, None),
        P("grp", "blk", None, None),
        P("grp", "blk", None),
    )
    out_specs = (P("grp", "blk", None, None, None), P("grp", "blk", None, None, None))
    body = functools.partial(local, mesh.shape["grp"], mesh.shape["blk"])
    return jax.shard_map(body, mesh=mesh, in_specs=in_specs, out_specs=out_specs, check_vma=False)
```

```python
import functools

import jax
import jax.numpy as jnp
from jax import lax
from jax.experimental import pallas as pl
from jax.experimental.pallas import tpu as pltpu
from jax.sharding import PartitionSpec as P

MESH = pl.DeviceIdType.MESH
HBM = pl.BlockSpec(memory_space=pl.ANY)


def remote(ref, first, length, send_sem, recv_sem, target):
    part = ref.at[pl.ds(first, length)]
    return pltpu.make_async_remote_copy(
        src_ref=part, dst_ref=part, send_sem=send_sem, recv_sem=recv_sem,
        device_id=target, device_id_type=MESH,
    )


def greet(targets):
    barrier = pltpu.get_barrier_semaphore()
    for present, target in targets:
        @pl.when(present)
        def _():
            pl.semaphore_signal(barrier, inc=1, device_id=target, device_id_type=MESH)
    total = sum(jnp.where(present, 1, 0) for present, _ in targets)
    pl.semaphore_wait(barrier, total)


class Group:
    def __init__(self, n_blk, cap):
        self.cap = cap
        self.g = lax.axis_index("grp")
        self.b = lax.axis_index("blk")
        self.chips = n_blk // 2
        self.q, self.core = self.b // 2, self.b % 2
        self.mate = (self.g, 2 * self.q + 1 - self.core)

    def peers(self):
        yes = self.b >= 0
        out = [(yes, self.mate)]
        for d in range(1, self.chips):
            out.append((yes, (self.g, self.chip(d))))
        return out

    def chip(self, d):
        return 2 * ((self.q + d) % self.chips) + self.core

    def source(self, d):
        return 2 * ((self.q + self.chips - d) % self.chips) + self.core

    def far(self, ref, sems, d, close=None):
        target = ref.at[pl.ds(self.b * self.cap, self.cap)]
        return pltpu.make_async_remote_copy(
            src_ref=target if close is None else close.at[pl.ds(self.core * self.cap, self.cap)],
            dst_ref=target, send_sem=sems[0].at[d], recv_sem=sems[1].at[d],
            device_id=(self.g, self.chip(d)), device_id_type=MESH,
        )

    def near(self, ref, sems, d, close=None):
        i = self.chips + d
        if d == 0 and close is not None:
            return remote(close, self.core * self.cap, self.cap, sems[0].at[i], sems[1].at[i], self.mate)
        return remote(ref, self.source(d) * self.cap, self.cap, sems[0].at[i], sems[1].at[i], self.mate)

    def start(self, ref, sems, close=None):
        for d in range(1, self.chips):
            self.far(ref, sems, d, close).start()
        self.near(ref, sems, 0, close).start()

    def forward(self, ref, sems):
        for d in range(1, self.chips):
            self.far(ref, sems, d).wait_recv()
            self.near(ref, sems, d).start()

    def finish(self, ref, sems, first=0):
        for d in range(first, self.chips):
            self.near(ref, sems, d).wait_recv()

    def finish_mate(self, close, sems):
        self.near(close, sems, 0, close).wait_recv()

    def drain(self, ref, sems, close=None):
        for d in range(1, self.chips):
            self.far(ref, sems, d, close).wait_send()
        for d in range(self.chips):
            self.near(ref, sems, d, close).wait_send()


class Panel:
    def __init__(self, n_grp, size):
        self.size = size
        self.b = lax.axis_index("blk")
        g = lax.axis_index("grp")
        self.nz = n_grp // 2
        self.z, self.x = g // 2, g % 2
        self.across = (2 * self.z + 1 - self.x, self.b)

    def peers(self):
        yes = self.b >= 0
        return [
            (self.z < self.nz - 1, self.at(self.z + 1)),
            (self.z > 0, self.at(self.z - 1)),
            (yes, self.across),
        ]

    def at(self, z):
        return (2 * z + self.x, self.b)

    def copy(self, ref, sems, i, z, target):
        first = (2 * z + self.x) * self.size
        return remote(ref, first, self.size, sems[0].at[i], sems[1].at[i], target)

    def line(self, ref, sems, way, k):
        step = 1 if way == 0 else -1
        return self.copy(ref, sems, way * self.nz + k, self.z - step * k, self.at(self.z + step))

    def cross(self, ref, sems, z):
        return self.copy(ref, sems, 2 * self.nz + z, z, self.across)

    def sends(self, way, k):
        if way == 0:
            return jnp.logical_and(self.z < self.nz - 1, self.z >= k)
        return jnp.logical_and(self.z > 0, self.nz - 1 - self.z >= k)

    def gets(self, way, k):
        return self.z >= k + 1 if way == 0 else self.nz - 1 - self.z >= k + 1

    def start(self, ref, sems):
        self.cross(ref, sems, self.z).start()
        for way in (0, 1):
            @pl.when(self.sends(way, 0))
            def _():
                self.line(ref, sems, way, 0).start()

    def step(self, ref, sems, k):
        for way in (0, 1):
            @pl.when(self.gets(way, k))
            def _():
                self.line(ref, sems, way, k).wait_recv()
                self.cross(ref, sems, self.z - (k + 1 if way == 0 else -(k + 1))).start()

                @pl.when(self.sends(way, k + 1))
                def _():
                    self.line(ref, sems, way, k + 1).start()

    def finish(self, ref, sems):
        for z in range(self.nz):
            self.cross(ref, sems, z).wait_recv()

    def drain(self, ref, sems):
        for z in range(self.nz):
            self.cross(ref, sems, z).wait_send()
        for k in range(self.nz):
            for way in (0, 1):
                @pl.when(self.sends(way, k))
                def _():
                    self.line(ref, sems, way, k).wait_send()


def add_products(acc, lists, sources, left_tile, right_tile):
    slot, pick, out, count = lists
    per = slot.shape[1]
    cap = acc.shape[0]

    number, device, start = sources

    def source(i, carry):
        c, first = device(i), start(i)
        total = count[0, c]
        sums = [acc[o] for o in range(cap)]
        for e in range(per):
            product = jnp.dot(
                left_tile(first + slot[c, e]), right_tile(pick[c, e]),
                preferred_element_type=jnp.float32,
            )
            enters = jnp.where(e < total, out[c, e], cap)
            for o in range(cap):
                sums[o] = sums[o] + jnp.where(enters == o, 1.0, 0.0) * product
        for o in range(cap):
            acc[o] = sums[o]
        return carry

    lax.fori_loop(0, number, source, 0)


def kernel(n_grp, n_blk, *refs):
    p_hbm, lists_hbm = refs[0], refs[1:5]
    square_hbm, new_hbm = refs[5:7]
    panels, left, halves, squares, cube = refs[7:9], refs[9], refs[10:12], refs[12:14], refs[14]
    closes = refs[-2:]
    lists = refs[15:19]
    ps, pr, gs, gr, local_sems = refs[19:-2]
    cap, bs, _ = p_hbm.shape
    w = bs // 2
    wide, group = Panel(n_grp, 2 * cap), Group(n_blk, cap)
    panel_sems = [(ps.at[j], pr.at[j]) for j in range(2)]
    group_sems = [(gs.at[j], gr.at[j]) for j in range(3)]

    own = pl.ds(group.b * cap, cap)
    fetch = pltpu.make_async_copy(p_hbm, left.at[own], local_sems.at[0])
    fetch.start()
    list_copies = [
        pltpu.make_async_copy(source, target, local_sems.at[1 + i])
        for i, (source, target) in enumerate(zip(lists_hbm, lists))
    ]
    for copy in list_copies:
        copy.start()
    fetch.wait()
    mine = left[own]
    first = (2 * wide.z + wide.x) * 2 * cap
    for j in range(2):
        panels[j][pl.ds(first, 2 * cap)] = mine[:, :, j * w:(j + 1) * w].reshape(2 * cap, w, w)
    greet(wide.peers() + group.peers())

    square_copies = []

    def square_chunk(j):
        wide.finish(panels[j], panel_sems[j])
        squares[j][...] = jnp.zeros_like(squares[j])
        add_products(
            squares[j], lists, (n_blk, lambda i: i, lambda i: i * cap), lambda i: left[i],
            lambda t: panels[j][pl.ds(2 * t, 2)].reshape(bs, w))
        closes[j][pl.ds(group.core * cap, cap)] = squares[j][...].astype(left.dtype)
        group.start(halves[j], group_sems[j], closes[j])
        square_copies.append(pltpu.make_async_copy(
            squares[j], square_hbm.at[:, :, pl.ds(j * w, w)], local_sems.at[5 + j]))
        square_copies[j].start()

    wide.start(panels[0], panel_sems[0])
    group.start(left, group_sems[2])
    for k in range(wide.nz - 1):
        wide.step(panels[0], panel_sems[0], k)
        if k == 0:
            wide.start(panels[1], panel_sems[1])
        else:
            wide.step(panels[1], panel_sems[1], k - 1)
    group.forward(left, group_sems[2])
    group.finish(left, group_sems[2])
    for copy in list_copies:
        copy.wait()
    square_chunk(0)
    wide.step(panels[1], panel_sems[1], wide.nz - 2)
    group.forward(halves[0], group_sems[0])
    square_chunk(1)
    cube[...] = jnp.zeros_like(cube)

    def right_whole(t):
        return jnp.concatenate(
            [panel[pl.ds(2 * t, 2)].reshape(bs, w) for panel in panels], axis=1)

    def left_whole(parts):
        return lambda i: jnp.concatenate([part[i] for part in parts], axis=1)

    for j in range(2):
        group.finish_mate(closes[j], group_sems[j])
    add_products(
        cube, lists, (2, lambda i: 2 * group.q + i, lambda i: i * cap),
        left_whole(closes), right_whole)
    group.forward(halves[1], group_sems[1])
    for j in range(2):
        group.finish(halves[j], group_sems[j], 1)

    def far_device(i):
        return 2 * ((group.q + 1 + i // 2) % group.chips) + i % 2

    add_products(
        cube, lists, (n_blk - 2, far_device, lambda i: far_device(i) * cap),
        left_whole(halves), right_whole)
    for j in range(2):
        cols = slice(j * w, (j + 1) * w)
        cube[:, :, cols] = 3.0 * squares[j][...] - 2.0 * cube[:, :, cols]
    last = pltpu.make_async_copy(cube, new_hbm, local_sems.at[7])
    last.start()
    for j in range(2):
        wide.drain(panels[j], panel_sems[j])
        square_copies[j].wait()
    for j in range(2):
        group.drain(halves[j], group_sems[j], closes[j])
    group.drain(left, group_sems[2])
    last.wait()


def local(n_grp, n_blk, p_tiles, pair_slot, pair_panel, pair_out, pair_count):
    held = p_tiles[0, 0]
    lists = (pair_slot[0, 0], pair_panel[0, 0], pair_out[0, 0], pair_count[0])
    cap, bs, _ = held.shape
    nz, chips, w = n_grp // 2, n_blk // 2, bs // 2
    dma = pltpu.SemaphoreType.DMA
    tile_type = jax.ShapeDtypeStruct((cap, bs, bs), jnp.float32)
    square, new = pl.pallas_call(
        functools.partial(kernel, n_grp, n_blk),
        out_shape=(tile_type, tile_type),
        in_specs=[HBM] * 5,
        out_specs=(HBM, HBM),
        scratch_shapes=[pltpu.VMEM((n_grp * cap * 2, w, w), held.dtype)] * 2
        + [pltpu.VMEM((n_blk * cap, bs, bs), held.dtype)]
        + [pltpu.VMEM((n_blk * cap, bs, w), held.dtype)] * 2
        + [pltpu.VMEM((cap, bs, w), jnp.float32)] * 2
        + [pltpu.VMEM((cap, bs, bs), jnp.float32)]
        + [pltpu.SMEM(x.shape, x.dtype) for x in lists]
        + [dma((2, 3 * nz))] * 2 + [dma((3, 2 * chips))] * 2 + [dma((8,))]
        + [pltpu.VMEM((2 * cap, bs, w), held.dtype)] * 2,
        compiler_params=pltpu.CompilerParams(
            collective_id=0, has_side_effects=True, vmem_limit_bytes=48 * 2**20),
    )(held, *lists)
    return square[None, None], new[None, None]


def solution(mesh):
    in_specs = (
        P("grp", "blk", None, None, None),
        P("grp", "blk", None, None),
        P("grp", "blk", None, None),
        P("grp", "blk", None, None),
        P("grp", "blk", None),
    )
    out_specs = (P("grp", "blk", None, None, None), P("grp", "blk", None, None, None))
    body = functools.partial(local, mesh.shape["grp"], mesh.shape["blk"])
    return jax.shard_map(body, mesh=mesh, in_specs=in_specs, out_specs=out_specs, check_vma=False)
```
